32 devices in a mesh: req: 8 (over z, y), mlp: 4 (over x, core).
Axes of the slice: x: 2, y: 2, z: 4, core: 2. Of those that a mesh axis runs over, the one named last changes fastest.
Arguments:
- tokens: bfloat16 [8192, 1536], P(('req', 'mlp')), may hold values from -6 to 6
- attn_gain: float32 [1536], replicated, may hold values from 0.1 to 1.9
- w_query: bfloat16 [1536, 1536], replicated, may hold values from -0.15625 to 0.15625
- w_keyval: bfloat16 [1536, 256], replicated, may hold values from -0.15625 to 0.15625
- w_out: bfloat16 [1536, 1536], replicated, may hold values from -0.15625 to 0.15625
- ffn_gain: float32 [1536], replicated, may hold values from 0.1 to 1.9
- w_gate: bfloat16 [1536, 4608], P('req', 'mlp'), may hold values from -0.15625 to 0.15625
- w_up: bfloat16 [1536, 4608], P('req', 'mlp'), may hold values from -0.15625 to 0.15625
- w_down: bfloat16 [1536, 4608], P('req', 'mlp'), may hold values from -0.09375 to 0.09375
- prefix_kv: bfloat16 [2, 64, 512, 256], P(None, 'req'), may hold values from -60 to 60, as said below
- own_prefix: bfloat16 [8, 512, 256], P('req'), may hold values from -60 to 60, as said below
- leaf_parent: int32 [8], replicated, may hold values from 0 to 63
- node_parent: int32 [64], replicated, may hold values from 0 to 63
- seg_lengths: int32 [3, 64], replicated, may hold values from 1 to 512
Outputs:
- layer_out: bfloat16 [8192, 1536], P(('req', 'mlp'))
The draws below stay inside these ranges and needn't reach their ends.
Inputs may be any that keep to these rules, and one draw needn't show every extreme that they name: `prefix_kv`: columns below 128 are keys, the rest values. `own_prefix`: columns below 128 are keys, the rest values.
All inputs are finite; a program needn't handle non-finite values.
Results may differ from the reference program's by a relative error of at most 0.018.
Values may be sent and summed in bfloat16 or wider, within the bound.
A program may use at most 192 MiB of HBM per device.

```python
import math
import jax
import jax.numpy as jnp
import numpy as np
from jax import lax

D = 1536
HEADS = 12
HD = 128
FF = 4608
WINDOW = 1024
SEG = 512
QTOK = 1024
REQS = 8
NODES = 64
TOKENS = 8192
N_MLP = 4


def kv_block(key, shape):
    key_one, key_two = jax.random.split(key, 2)
    half_shape = shape[:-1] + (HD,)
    keys_part = jax.random.normal(key_one, half_shape, jnp.float32)
    vals_part = jax.random.normal(key_two, half_shape, jnp.float32)
    return jnp.clip(jnp.concatenate([keys_part, vals_part], -1), -60.0, 60.0).astype(jnp.bfloat16)


def draw_prefix_kv(key, part):
    return kv_block(jax.random.fold_in(key, 11), (2, NODES, SEG, 2 * HD))


def draw_own_prefix(key, part):
    return kv_block(jax.random.fold_in(key, 23), (REQS, SEG, 2 * HD))


def touch_ends(result, stream_key, low, high):
    place = [jax.random.randint(jax.random.fold_in(stream_key, axis), (), 0, length) for axis, length in enumerate(result.shape)]
    main_axis = result.shape.index(max(result.shape))
    beside = place[:main_axis] + [(place[main_axis] + 1) % result.shape[main_axis]] + place[main_axis + 1:]
    return result.at[tuple(place)].set(low).at[tuple(beside)].set(high)


def shard_levels(key, dims, pieces, smallest, top_value):
    factor_of = 1.0
    for dim, blocks in pieces:
        draws = jax.random.uniform(jax.random.fold_in(jax.random.fold_in(key, 6), dim), (blocks,), jnp.float32, smallest / len(pieces), top_value / len(pieces))
        factor_of = factor_of * jnp.repeat(jnp.exp(draws), dims[dim] // blocks).reshape((-1,) + (1,) * (len(dims) - 1 - dim))
    return factor_of


def rank_table(count, slope):
    portions = [(1 << 20) // math.isqrt(grade ** slope) + 1 for grade in range(1, count + 1)]
    spread = 1 + sum(portions) // (1 << 30)
    return np.cumsum(np.array([max(1, weight // spread) for weight in portions]))


def ranked(stream_key, extent, amount, slope):
    listing = rank_table(amount, slope)
    pick = jax.random.randint(jax.random.fold_in(stream_key, 1), extent, 0, int(listing[amount - 1]))
    standing = jnp.searchsorted(jnp.asarray(listing, jnp.int32), pick, side="right")
    return jax.random.permutation(jax.random.fold_in(stream_key, 2), amount)[standing].astype(jnp.int32)


def bell_draw(key, extent, spread, most, cuts=(), held_as=jnp.bfloat16):
    drawn = jax.random.normal(key, extent, jnp.float32) * spread
    if len(cuts) > 0:
        drawn = shard_levels(key, extent, cuts, -0.22, 0.18) * drawn
    return jnp.clip(drawn, min=-most, max=most).astype(held_as)


def setup_inputs(seed: int = 0) -> dict:
    splits = jax.random.split(jax.random.key(seed), 15)
    return {
        "tokens": bell_draw(splits[0], (TOKENS, D), 1.0, 6.0, ((0, 32),)),
        "attn_gain": jnp.clip(1.0 + 0.18 * jax.random.normal(splits[1], (D,), jnp.float32), 0.1, 1.9),
        "w_query": bell_draw(splits[2], (D, HEADS * HD), D ** -0.5, 0.15625),
        "w_keyval": bell_draw(splits[3], (D, 2 * HD), D ** -0.5, 0.15625),
        "w_out": bell_draw(splits[4], (HEADS * HD, D), (HEADS * HD) ** -0.5, 0.15625),
        "ffn_gain": jnp.clip(1.0 + 0.18 * jax.random.normal(splits[5], (D,), jnp.float32), 0.1, 1.9),
        "w_gate": bell_draw(splits[6], (D, FF), D ** -0.5, 0.15625, ((0, 8), (1, 4))),
        "w_up": bell_draw(splits[7], (D, FF), D ** -0.5, 0.15625, ((0, 8), (1, 4))),
        "w_down": bell_draw(splits[8], (D, FF), FF ** -0.5, 0.09375, ((0, 8), (1, 4))),
        "prefix_kv": draw_prefix_kv(jax.random.fold_in(splits[14], 71), 0),
        "own_prefix": draw_own_prefix(jax.random.fold_in(splits[14], 71), 0),
        "leaf_parent": touch_ends(ranked(splits[11], (REQS,), NODES, 2), jax.random.fold_in(splits[11], 3), 0, NODES - 1).astype(jnp.int32),
        "node_parent": touch_ends(ranked(splits[12], (NODES,), NODES, 2), jax.random.fold_in(splits[12], 3), 0, NODES - 1).astype(jnp.int32),
        "seg_lengths": touch_ends(jax.random.randint(splits[13], (3, NODES), 1, SEG + 1), jax.random.fold_in(splits[13], 1), 1, SEG).astype(jnp.int32),
    }


EPS = 1e-06

def rounded(values):
    return lax.optimization_barrier(values.astype(jnp.bfloat16))

def rms_scale(values, gain):
    wide = values.astype(jnp.float32)
    return wide * lax.rsqrt(lax.optimization_barrier(jnp.mean(wide * wide, axis=-1, keepdims=True)) + EPS) * gain

def rotate(values, where_at):
    half_dim = values.shape[-1] // 2
    freqs = 10000.0 ** (-jnp.arange(half_dim, dtype=jnp.float32) / half_dim)
    angles = where_at.astype(jnp.float32)[:, None] * freqs[None, :]
    cosine = jnp.cos(angles)[:, None, :]
    sine = jnp.sin(angles)[:, None, :]
    first = values[..., :half_dim]
    second = values[..., half_dim:]
    return jnp.concatenate([first * cosine - second * sine, first * sine + second * cosine], -1)

def reference(tokens, attn_gain, w_query, w_keyval, w_out, ffn_gain, w_gate, w_up, w_down, prefix_kv, own_prefix, leaf_parent, node_parent, seg_lengths):
    normed = rounded(rms_scale(tokens, attn_gain))
    query_all = jnp.dot(normed, w_query, preferred_element_type=jnp.float32)
    keyval_all = jnp.dot(normed, w_keyval, preferred_element_type=jnp.float32)
    offsets = jnp.arange(SEG, dtype=jnp.int32)
    steps_new = jnp.arange(QTOK, dtype=jnp.int32)

    def one_request(request):
        leaf = leaf_parent[request]
        upper = node_parent[leaf]
        len_zero = seg_lengths[0, upper]
        len_one = seg_lengths[1, leaf]
        len_two = seg_lengths[2, request]
        total = len_zero + len_one + len_two
        query_at = total + steps_new
        start_row = (request * QTOK).astype(jnp.int32)
        rows_query = lax.dynamic_slice_in_dim(query_all, start_row, QTOK, 0).reshape(QTOK, HEADS, HD)
        queries = rounded(rotate(rows_query, query_at) * HD ** (-0.5))
        rows_keyval = lax.dynamic_slice_in_dim(keyval_all, start_row, QTOK, 0)
        new_keys = rounded(rotate(rows_keyval[:, None, :HD], query_at)[:, 0])
        new_vals = rounded(rows_keyval[:, HD:])
        cached = jnp.concatenate([prefix_kv[0, upper], prefix_kv[1, leaf], own_prefix[request]], 0)
        key_rows = jnp.concatenate([cached[:, :HD], new_keys], 0)
        val_rows = jnp.concatenate([cached[:, HD:], new_vals], 0)
        key_at = jnp.concatenate([offsets, len_zero + offsets, len_zero + len_one + offsets, query_at], 0)
        key_live = jnp.concatenate([offsets < len_zero, offsets < len_one, offsets < len_two, jnp.ones((QTOK,), dtype=bool)], 0)
        scores = jnp.einsum('thd,kd->thk', queries.astype(jnp.float32), key_rows.astype(jnp.float32))
        spacing = query_at[:, None] - key_at[None, :]
        allowed = (key_live[None, :] & (spacing >= 0) & (spacing < WINDOW))[:, None, :]
        top = lax.optimization_barrier(jnp.max(jnp.where(allowed, scores, -jnp.inf), axis=-1, keepdims=True))
        weights = jnp.where(allowed, jnp.exp(scores - top), 0.0)
        denom = lax.optimization_barrier(jnp.sum(weights, axis=-1))
        mixed = jnp.einsum('thk,kd->thd', rounded(weights).astype(jnp.float32), val_rows.astype(jnp.float32))
        return (mixed / denom[..., None]).reshape(QTOK, HEADS * HD).astype(jnp.bfloat16)
    contexts = lax.map(one_request, jnp.arange(REQS, dtype=jnp.int32)).reshape(TOKENS, HEADS * HD)
    attn_out = jnp.dot(contexts, w_out, preferred_element_type=jnp.float32)
    resid = rounded(tokens.astype(jnp.float32) + attn_out)
    ffn_in = rounded(rms_scale(resid, ffn_gain))
    gate = jnp.dot(ffn_in, w_gate, preferred_element_type=jnp.float32)
    upward = jnp.dot(ffn_in, w_up, preferred_element_type=jnp.float32)
    hidden = rounded(jax.nn.gelu(gate, approximate=True) * upward)
    slice_width = FF // N_MLP

    def add_slice(summed, index):
        first_col = (index * slice_width).astype(jnp.int32)
        cols = lax.dynamic_slice_in_dim(hidden, first_col, slice_width, 1)
        down_cols = lax.dynamic_slice_in_dim(w_down, first_col, slice_width, 1)
        partial_sum = lax.dot_general(cols, down_cols, (((1,), (1,)), ((), ())), preferred_element_type=jnp.float32)
        return (summed + rounded(partial_sum).astype(jnp.float32), None)
    summed, unused = lax.scan(add_slice, jnp.zeros((TOKENS, D), jnp.float32), jnp.arange(N_MLP, dtype=jnp.int32))
    return (resid.astype(jnp.float32) + summed).astype(jnp.bfloat16)
```

```python
import functools

import jax
import jax.numpy as jnp
from jax import lax
from jax.experimental import pallas as pl
from jax.experimental.pallas import tpu as pltpu
from jax.sharding import PartitionSpec as P

HEADS = 12
HD = 128
WINDOW = 1024


EPS = 1e-06


def rms_scale(values, gain):
    wide = values.astype(jnp.float32)
    return wide * lax.rsqrt(jnp.mean(wide * wide, axis=-1, keepdims=True) + EPS) * gain


def rotate(values, where_at):
    half_dim = values.shape[-1] // 2
    freqs = 10000.0 ** (-jnp.arange(half_dim, dtype=jnp.float32) / half_dim)
    angles = where_at.astype(jnp.float32)[:, None] * freqs[None, :]
    cosine = jnp.cos(angles)[:, None, :]
    sine = jnp.sin(angles)[:, None, :]
    first = values[..., :half_dim]
    second = values[..., half_dim:]
    return jnp.concatenate([first * cosine - second * sine, first * sine + second * cosine], -1)


LINE = 4
MASKED = -1e30


def layer_kernel(
    dims, q_ref, kv_ref, ok_ref, tok_ref, gain_ref, wout_hbm, wg_hbm, wu_hbm, wd_hbm, out_ref,
    w_all, w_out, bias, ctx, rows_all, hidden, part, landed,
    load_sem, zs, zr, ys, yr, ts, tr, ps, pr,
):
    n_req, n_mlp = dims
    cross = n_req // LINE
    me, mine = lax.axis_index("req"), lax.axis_index("mlp")
    za, yb = me // cross, me % cross
    depth = wg_hbm.shape[0]
    tok = tok_ref.shape[0]
    model = tok_ref.shape[1]
    chunk = model // LINE
    keys = kv_ref.shape[0]

    loads = [
        pltpu.make_async_copy(ref, w_all.at[w, pl.ds(pl.multiple_of(me * depth, 16), depth)], load_sem.at[w])
        for w, ref in enumerate((wg_hbm, wu_hbm, wd_hbm))
    ]
    loads.append(pltpu.make_async_copy(wout_hbm, w_out, load_sem.at[3]))
    for load in loads:
        load.start()

    barrier = pltpu.get_barrier_semaphore()
    for k in range(1, LINE):
        pl.semaphore_signal(barrier, inc=1, device_id={"req": ((za + k) % LINE) * cross + yb})
    for k in range(1, cross):
        pl.semaphore_signal(barrier, inc=1, device_id={"req": za * cross + (yb + k) % cross})
    for k in range(1, n_mlp):
        pl.semaphore_signal(barrier, inc=1, device_id={"mlp": (mine + k) % n_mlp})
    pl.semaphore_wait(barrier, LINE + cross + n_mlp - 3)

    def block(w, a, b):
        return w_all.at[w, pl.ds(pl.multiple_of((a * cross + b) * depth, 16), depth)]

    def z_copy(w, a, toward, side):
        return pltpu.make_async_remote_copy(
            src_ref=block(w, a, yb), dst_ref=block(w, a, yb),
            send_sem=zs.at[w, a, side], recv_sem=zr.at[w, a],
            device_id={"req": toward * cross + yb},
        )

    def y_copy(w, a, b, toward, side):
        return pltpu.make_async_remote_copy(
            src_ref=block(w, a, b), dst_ref=block(w, a, b),
            send_sem=ys.at[w, a, b, side], recv_sem=yr.at[w, a, b],
            device_id={"req": za * cross + toward},
        )

    def y_send(w, a, b, steps, finish=False):
        for step in steps:
            @pl.when((yb + step >= 0) & (yb + step < cross))
            def _():
                copy = y_copy(w, a, b, yb + step, (step + 1) // 2)
                copy.wait_send() if finish else copy.start()

    def z_send(w, a, steps, finish=False):
        for step in steps:
            @pl.when((za + step >= 0) & (za + step < LINE))
            def _():
                copy = z_copy(w, a, za + step, (step + 1) // 2)
                copy.wait_send() if finish else copy.start()

    def own(w, finish=False):
        z_send(w, za, (-1, 1), finish)
        y_send(w, za, yb, (-1, 1), finish)

    def relay(w, dist, finish=False):
        for side in (-1, 1):
            origin = za + side * dist

            @pl.when((origin >= 0) & (origin < LINE))
            def _():
                if not finish:
                    z_copy(w, origin, za, 0).wait_recv()
                z_send(w, origin, (-side,), finish)
                y_send(w, origin, yb, (-1, 1), finish)

    def y_wait(w, a):
        for dist in range(1, cross):
            for side in (-1, 1):
                origin = yb + side * dist

                @pl.when((origin >= 0) & (origin < cross))
                def _():
                    y_copy(w, a, origin, yb, 0).wait_recv()
                    y_send(w, a, origin, (-side,))

    for load in loads[:3]:
        load.wait()
    own(0)
    own(1)

    query_row = lax.broadcasted_iota(jnp.int32, (tok, keys), 0)
    slot = lax.broadcasted_iota(jnp.int32, (tok, keys), 1)
    allowed = (slot > query_row) & (slot <= query_row + WINDOW) & (ok_ref[...] > 0)
    bias[...] = jnp.where(allowed, 0.0, MASKED)

    def heads(first, count):
        @pl.loop(first, first + count)
        def _(h):
            cols = pl.ds(pl.multiple_of(h * HD, HD), HD)
            scores = lax.dot_general(
                q_ref[:, cols], kv_ref[:, :HD], (((1,), (1,)), ((), ())),
                preferred_element_type=jnp.float32,
            ) + bias[...]
            weights = jnp.exp(scores - jnp.max(scores, axis=-1, keepdims=True))
            denom = jnp.sum(weights, axis=-1, keepdims=True)
            mixed = jnp.dot(
                weights.astype(jnp.bfloat16), kv_ref[:, HD:], preferred_element_type=jnp.float32
            )
            ctx[:, cols] = (mixed / denom).astype(jnp.bfloat16)

    third = HEADS // 3
    heads(0, third)
    relay(0, 1)
    heads(third, third)
    relay(1, 1)
    own(2)
    heads(2 * third, HEADS - 2 * third)
    relay(0, 2)
    loads[3].wait()

    @pl.loop(0, LINE)
    def _(c):
        cols = pl.ds(pl.multiple_of(c * chunk, 128), chunk)
        out_ref[:, cols] = (
            tok_ref[:, cols].astype(jnp.float32)
            + jnp.dot(ctx[...], w_out[:, cols], preferred_element_type=jnp.float32)
        ).astype(jnp.bfloat16)

    rows_all[mine] = rms_scale(out_ref[...], gain_ref[...]).astype(jnp.bfloat16)

    def t_copy(owner, toward):
        return pltpu.make_async_remote_copy(
            src_ref=rows_all.at[owner], dst_ref=rows_all.at[owner],
            send_sem=ts.at[toward], recv_sem=tr.at[owner], device_id={"mlp": toward},
        )

    others = [(mine + k) % n_mlp for k in range(1, n_mlp)]
    for toward in others:
        t_copy(mine, toward).start()
    relay(1, 2)
    relay(2, 1)
    relay(0, 3)
    relay(1, 3)
    relay(2, 2)
    for w in range(2):
        for a in range(LINE):
            y_wait(w, a)

    width = hidden.shape[2]
    tile = 384 if width % 384 == 0 else width

    def gate_up(g):
        for c in range(width // tile):
            cols = pl.ds(c * tile, tile)
            gate = jnp.dot(rows_all[g], w_all[0, :, cols], preferred_element_type=jnp.float32)
            upward = jnp.dot(rows_all[g], w_all[1, :, cols], preferred_element_type=jnp.float32)
            hidden[g, :, cols] = (jax.nn.gelu(gate, approximate=True) * upward).astype(jnp.bfloat16)

    @pl.loop(0, n_mlp)
    def _(k):
        g = (mine + k) % n_mlp

        @pl.when(k > 0)
        def _():
            t_copy(g, mine).wait_recv()

        gate_up(g)

    relay(2, 3)

    def p_copy(g, src, c):
        return pltpu.make_async_remote_copy(
            src_ref=part.at[g, c], dst_ref=landed.at[src, c],
            send_sem=ps.at[g, c], recv_sem=pr.at[src, c], device_id={"mlp": g},
        )

    def nth(k):
        second = jnp.where(za == 0, 1, za - 1)
        third_a = jnp.where(za == 3, 1, jnp.where(za == 2, 3, 2))
        fourth = jnp.where(za < 2, 3, 0)
        return jnp.where(k == 0, za, jnp.where(k == 1, second, jnp.where(k == 2, third_a, fourth)))

    @pl.loop(0, LINE)
    def _(k):
        a = nth(k)
        y_wait(2, a)

        @pl.loop(1, n_mlp + 1)
        def _(j):
            g = (mine + j) % n_mlp
            part[g, a] = lax.dot_general(
                hidden[g], w_all[2, pl.ds(pl.multiple_of(a * chunk, 16), chunk)],
                (((1,), (1,)), ((), ())), preferred_element_type=jnp.float32,
            ).astype(jnp.bfloat16)

            @pl.when(j < n_mlp)
            def _():
                p_copy(g, mine, a).start()

    @pl.loop(0, LINE)
    def _(k):
        a = nth(k)
        cols = pl.ds(pl.multiple_of(a * chunk, 128), chunk)
        total = part[mine, a].astype(jnp.float32)
        for g in others:
            p_copy(mine, g, a).wait_recv()
            total = total + landed[g, a].astype(jnp.float32)
        out_ref[:, cols] = (out_ref[:, cols].astype(jnp.float32) + total).astype(jnp.bfloat16)

    for toward in others:
        t_copy(mine, toward).wait_send()

    @pl.loop(0, LINE)
    def _(a):
        for g in others:
            p_copy(g, mine, a).wait_send()

    @pl.loop(0, 3)
    def _(w):
        own(w, True)
        for dist in range(1, LINE):
            relay(w, dist, True)

        @pl.loop(0, LINE)
        def _(a):
            for dist in range(1, cross):
                for side in (-1, 1):
                    origin = yb + side * dist

                    @pl.when((origin >= 0) & (origin < cross))
                    def _():
                        y_send(w, a, origin, (-side,), True)


def fused_layer(n_req, n_mlp, q, kv, ok, tokens, gain, w_out, w_gate, w_up, w_down):
    tok, model = tokens.shape
    depth, width = w_gate.shape
    chunk = model // LINE
    cross = n_req // LINE
    whole = pl.BlockSpec(memory_space=pltpu.VMEM)
    far = pl.BlockSpec(memory_space=pl.ANY)
    dma = pltpu.SemaphoreType.DMA
    half = jnp.bfloat16
    return pl.pallas_call(
        functools.partial(layer_kernel, (n_req, n_mlp)),
        out_shape=jax.ShapeDtypeStruct((tok, model), half),
        in_specs=[whole] * 5 + [far] * 4,
        out_specs=whole,
        scratch_shapes=[
            pltpu.VMEM((3, model, width), half),
            pltpu.VMEM(w_out.shape, half),
            pltpu.VMEM((tok, kv.shape[0]), jnp.float32),
            pltpu.VMEM((tok, HEADS * HD), half),
            pltpu.VMEM((n_mlp, tok, model), half),
            pltpu.VMEM((n_mlp, tok, width), half),
            pltpu.VMEM((n_mlp, LINE, tok, chunk), half),
            pltpu.VMEM((n_mlp, LINE, tok, chunk), half),
            dma((4,)),
            dma((3, LINE, 2)),
            dma((3, LINE)),
            dma((3, LINE, cross, 2)),
            dma((3, LINE, cross)),
            dma((n_mlp,)),
            dma((n_mlp,)),
            dma((n_mlp, LINE)),
            dma((n_mlp, LINE)),
        ],
        compiler_params=pltpu.CompilerParams(
            collective_id=0, has_side_effects=True, vmem_limit_bytes=58 * 1024 * 1024
        ),
    )(q, kv, ok, tokens, gain, w_out, w_gate, w_up, w_down)


def body(
    tokens, attn_gain, w_query, w_keyval, w_out, ffn_gain, w_gate, w_up, w_down,
    prefix_kv, own_prefix, leaf_parent, node_parent, seg_lengths,
):
    tok_rows = tokens.shape[0]
    requests = lax.axis_size("req")
    groups = lax.axis_size("mlp")
    mine = lax.axis_index("req")
    position_group = lax.axis_index("mlp")
    node_dev = prefix_kv.shape[1]
    seg_slot = prefix_kv.shape[2]
    leaf = leaf_parent[mine]
    upper = node_parent[leaf]
    len_zero = seg_lengths[0, upper]
    len_one = seg_lengths[1, leaf]
    len_two = seg_lengths[2, mine]
    total = len_zero + len_one + len_two

    share = seg_slot // groups
    level_zero = node_parent[leaf_parent]
    wanted = jnp.stack([level_zero, leaf_parent], 1)
    owned = wanted // node_dev == mine
    local_slot = wanted % node_dev
    picker = (
        (local_slot[:, :, None] == jnp.arange(node_dev, dtype=jnp.int32)[None, None, :])
        & owned[:, :, None]
    ).astype(jnp.bfloat16)
    owners = wanted[mine] // node_dev
    from_owner = (jnp.arange(requests, dtype=jnp.int32)[:, None] == owners[None, :]).astype(
        jnp.bfloat16
    )
    shared_rows = lax.dynamic_slice_in_dim(prefix_kv, position_group * share, share, 2)
    outgoing = jnp.einsum(
        "rln,lnsc->rlsc", picker, shared_rows, preferred_element_type=jnp.float32
    ).astype(jnp.bfloat16)
    arrived = lax.all_to_all(outgoing, "req", split_axis=0, concat_axis=0, tiled=True)

    query_at = total + position_group * tok_rows + jnp.arange(tok_rows, dtype=jnp.int32)
    normed = rms_scale(tokens, attn_gain).astype(jnp.bfloat16)
    keyval_full = jnp.dot(normed, w_keyval, preferred_element_type=jnp.float32)
    new_keys = rotate(keyval_full[:, None, :HD], query_at)[:, 0].astype(jnp.bfloat16)
    new_vals = keyval_full[:, HD:].astype(jnp.bfloat16)
    new_keyval = jnp.concatenate([new_keys, new_vals], 1)
    query_full = jnp.dot(normed, w_query, preferred_element_type=jnp.float32).reshape(
        tok_rows, HEADS, HD
    )
    queries = (rotate(query_full, query_at) * HD ** (-0.5)).astype(jnp.bfloat16)

    levels = jnp.einsum(
        "rl,rlsc->lsc", from_owner, arrived, preferred_element_type=jnp.float32
    ).astype(jnp.bfloat16)
    gathered = lax.all_gather(
        jnp.concatenate([levels[0], levels[1], new_keyval], 0), "mlp", axis=0
    )
    cached = gathered[:, : 2 * share].reshape(groups, 2, share, 2 * HD)
    laid = jnp.zeros((WINDOW + 3 * seg_slot + groups * tok_rows, 2 * HD), jnp.bfloat16)
    laid = lax.dynamic_update_slice(laid, cached[:, 0].reshape(seg_slot, 2 * HD), (WINDOW, 0))
    laid = lax.dynamic_update_slice(
        laid, cached[:, 1].reshape(seg_slot, 2 * HD), (WINDOW + len_zero, 0)
    )
    laid = lax.dynamic_update_slice(laid, own_prefix[0], (WINDOW + len_zero + len_one, 0))
    laid = lax.dynamic_update_slice(
        laid, gathered[:, 2 * share :].reshape(groups * tok_rows, 2 * HD), (WINDOW + total, 0)
    )
    first = total + position_group * tok_rows
    keys = WINDOW + tok_rows
    window = lax.dynamic_slice_in_dim(laid, first, keys, 0)
    used = (first - WINDOW + jnp.arange(keys, dtype=jnp.int32) >= 0).astype(jnp.int32)[None, :]
    return fused_layer(
        requests, groups, queries.reshape(tok_rows, HEADS * HD), window, used, tokens,
        ffn_gain[None, :], w_out, w_gate, w_up, w_down,
    )


def solution(mesh):
    return jax.shard_map(
        body,
        mesh=mesh,
        in_specs=(
            P(("req", "mlp"), None),
            P(),
            P(),
            P(),
            P(),
            P(),
            P("req", "mlp"),
            P("req", "mlp"),
            P("req", "mlp"),
            P(None, "req", None, None),
            P("req", None, None),
            P(),
            P(),
            P(),
        ),
        out_specs=P(("req", "mlp"), None),
        check_vma=False,
    )
```

```python
import functools

import jax
import jax.numpy as jnp
from jax import lax
from jax.experimental import pallas as pl
from jax.experimental.pallas import tpu as pltpu
from jax.sharding import PartitionSpec as P

HEADS = 12
HD = 128
WINDOW = 1024


EPS = 1e-06


def rms_scale(values, gain):
    wide = values.astype(jnp.float32)
    return wide * lax.rsqrt(jnp.mean(wide * wide, axis=-1, keepdims=True) + EPS) * gain


def rotate(values, where_at):
    half_dim = values.shape[-1] // 2
    freqs = 10000.0 ** (-jnp.arange(half_dim, dtype=jnp.float32) / half_dim)
    angles = where_at.astype(jnp.float32)[:, None] * freqs[None, :]
    cosine = jnp.cos(angles)[:, None, :]
    sine = jnp.sin(angles)[:, None, :]
    first = values[..., :half_dim]
    second = values[..., half_dim:]
    return jnp.concatenate([first * cosine - second * sine, first * sine + second * cosine], -1)


LINE = 4
MASKED = -1e30
N_EARLY = 10


def layer_kernel(
    dims, q_ref, kv_ref, ok_ref, tok_ref, gain_ref, wout_hbm, wg_hbm, wu_hbm, wd_hbm, *rest
):
    early, rest = rest[:N_EARLY * dims[2]], rest[N_EARLY * dims[2]:]
    layer_steps(
        dims[:2], early, q_ref, kv_ref, ok_ref, tok_ref, gain_ref, wout_hbm, wg_hbm, wu_hbm,
        wd_hbm, *rest
    )


def layer_steps(
    dims, early, q_ref, kv_ref, ok_ref, tok_ref, gain_ref, wout_hbm, wg_hbm, wu_hbm, wd_hbm,
    out_ref, w_all, w_out, bias, ctx, rows_all, hidden, part, landed,
    load_sem, zs, zr, ys, yr, ts, tf, tr, ps, pr,
):
    n_req, n_mlp = dims
    cross = n_req // LINE
    me, mine = lax.axis_index("req"), lax.axis_index("mlp")
    za, yb = me // cross, me % cross
    depth = wg_hbm.shape[0]
    tok = tok_ref.shape[0]
    model = tok_ref.shape[1]
    chunk = model // LINE
    keys = kv_ref.shape[0]

    loads = [
        pltpu.make_async_copy(ref, w_all.at[w, pl.ds(pl.multiple_of(me * depth, 16), depth)], load_sem.at[w])
        for w, ref in enumerate((wg_hbm, wu_hbm, wd_hbm))
    ]
    loads.append(pltpu.make_async_copy(wout_hbm, w_out, load_sem.at[3]))
    for load in loads:
        load.start()

    ready = []
    for i, src in enumerate(early):
        kind = EARLY_BLOCKS[i]
        for j in range(src.shape[0]):
            a, b = za + kind[1], (1 - yb if kind[2] else yb)
            place = jnp.clip(a, 0, LINE - 1) * cross + b
            copy = pltpu.make_async_copy(
                src.at[j],
                w_all.at[kind[0] + j, pl.ds(pl.multiple_of(place * depth, 16), depth)],
                load_sem.at[4 + 2 * i + j],
            )
            ready.append(((a >= 0) & (a < LINE), copy))
    for there, copy in ready:
        @pl.when(there)
        def _():
            copy.start()

    barrier = pltpu.get_barrier_semaphore()
    for k in range(1, LINE):
        pl.semaphore_signal(barrier, inc=1, device_id={"req": ((za + k) % LINE) * cross + yb})
    for k in range(1, cross):
        pl.semaphore_signal(barrier, inc=1, device_id={"req": za * cross + (yb + k) % cross})
    for k in range(1, n_mlp):
        pl.semaphore_signal(barrier, inc=1, device_id={"mlp": (mine + k) % n_mlp})
    pl.semaphore_wait(barrier, LINE + cross + n_mlp - 3)

    def block(w, a, b):
        return w_all.at[w, pl.ds(pl.multiple_of((a * cross + b) * depth, 16), depth)]

    def z_copy(w, a, toward, side):
        return pltpu.make_async_remote_copy(
            src_ref=block(w, a, yb), dst_ref=block(w, a, yb),
            send_sem=zs.at[w, a, side], recv_sem=zr.at[w, a],
            device_id={"req": toward * cross + yb},
        )

    def y_copy(w, a, b, toward, side):
        return pltpu.make_async_remote_copy(
            src_ref=block(w, a, b), dst_ref=block(w, a, b),
            send_sem=ys.at[w, a, b, side], recv_sem=yr.at[w, a, b],
            device_id={"req": za * cross + toward},
        )

    def y_send(w, a, b, steps, finish=False):
        for step in steps:
            @pl.when((yb + step >= 0) & (yb + step < cross))
            def _():
                copy = y_copy(w, a, b, yb + step, (step + 1) // 2)
                copy.wait_send() if finish else copy.start()

    def z_send(w, a, steps, finish=False):
        for step in steps:
            @pl.when((za + step >= 0) & (za + step < LINE))
            def _():
                copy = z_copy(w, a, za + step, (step + 1) // 2)
                copy.wait_send() if finish else copy.start()

    def own(w, finish=False):
        z_send(w, za, (-1, 1), finish)
        y_send(w, za, yb, (-1, 1), finish)

    def relay(w, dist, finish=False):
        for side in (-1, 1):
            origin = za + side * dist

            @pl.when((origin >= 0) & (origin < LINE))
            def _():
                if not (finish or (early and (dist == 1 or (w == 0 and dist == 2)))):
                    z_copy(w, origin, za, 0).wait_recv()
                z_send(w, origin, (-side,), finish)
                y_send(w, origin, yb, (-1, 1), finish)

    def y_wait(w, a):
        if early:
            @pl.when(jnp.abs(a - za) > (1 if w == 0 else 0))
            def _():
                y_copy(w, a, 1 - yb, yb, 0).wait_recv()
            return
        for dist in range(1, cross):
            for side in (-1, 1):
                origin = yb + side * dist

                @pl.when((origin >= 0) & (origin < cross))
                def _():
                    y_copy(w, a, origin, yb, 0).wait_recv()
                    y_send(w, a, origin, (-side,))

    for load in loads[:3]:
        load.wait()
    for there, copy in ready:
        @pl.when(there)
        def _():
            copy.wait()
    if early:
        relay(1, 1)
        relay(0, 2)
    else:
        own(0)
        own(1)

    query_row = lax.broadcasted_iota(jnp.int32, (tok, keys), 0)
    slot = lax.broadcasted_iota(jnp.int32, (tok, keys), 1)
    allowed = (slot > query_row) & (slot <= query_row + WINDOW) & (ok_ref[...] > 0)
    bias[...] = jnp.where(allowed, 0.0, MASKED)

    def heads(first, count):
        @pl.loop(first, first + count)
        def _(h):
            cols = pl.ds(pl.multiple_of(h * HD, HD), HD)
            scores = lax.dot_general(
                q_ref[:, cols], kv_ref[:, :HD], (((1,), (1,)), ((), ())),
                preferred_element_type=jnp.float32,
            ) + bias[...]
            weights = jnp.exp(scores - jnp.max(scores, axis=-1, keepdims=True))
            denom = jnp.sum(weights, axis=-1, keepdims=True)
            mixed = jnp.dot(
                weights.astype(jnp.bfloat16), kv_ref[:, HD:], preferred_element_type=jnp.float32
            )
            ctx[:, cols] = (mixed / denom).astype(jnp.bfloat16)

    third = HEADS // 3
    heads(0, third)
    if early:
        relay(2, 1)
    else:
        relay(0, 1)
        relay(1, 1)
    heads(third, third)
    if early:
        relay(1, 2)
    else:
        own(2)
        relay(0, 2)
    heads(2 * third, HEADS - 2 * third)
    relay(0, 3) if early else relay(1, 2)
    loads[3].wait()

    @pl.loop(0, LINE)
    def _(c):
        cols = pl.ds(pl.multiple_of(c * chunk, 128), chunk)
        out_ref[:, cols] = (
            tok_ref[:, cols].astype(jnp.float32)
            + jnp.dot(ctx[...], w_out[:, cols], preferred_element_type=jnp.float32)
        ).astype(jnp.bfloat16)

    rows_all[mine] = rms_scale(out_ref[...], gain_ref[...]).astype(jnp.bfloat16)

    def t_copy(owner, toward, sem):
        return pltpu.make_async_remote_copy(
            src_ref=rows_all.at[owner], dst_ref=rows_all.at[owner],
            send_sem=sem, recv_sem=tr.at[owner], device_id={"mlp": toward},
        )

    others = [(mine + k) % n_mlp for k in range(1, n_mlp)]
    core = mine % 2
    sibling = mine + 1 - 2 * core
    alike = [(mine + 2 * k) % n_mlp for k in range(1, n_mlp // 2)]
    for toward in alike + [sibling]:
        t_copy(mine, toward, ts.at[toward]).start()
    if early:
        relay(2, 2)
        relay(1, 3)
    else:
        relay(2, 1)
        relay(0, 3)
        relay(1, 3)
        relay(2, 2)
    for owner in alike:
        t_copy(owner, mine, ts.at[0]).wait_recv()
        t_copy(owner, sibling, tf.at[owner]).start()
    for w in range(2):
        for a in range(LINE):
            y_wait(w, a)

    width = hidden.shape[2]
    tile = 384 if width % 384 == 0 else width

    def gate_up(g):
        for c in range(width // tile):
            cols = pl.ds(c * tile, tile)
            gate = jnp.dot(rows_all[g], w_all[0, :, cols], preferred_element_type=jnp.float32)
            upward = jnp.dot(rows_all[g], w_all[1, :, cols], preferred_element_type=jnp.float32)
            hidden[g, :, cols] = (jax.nn.gelu(gate, approximate=True) * upward).astype(jnp.bfloat16)

    gate_up(mine)
    for g in alike:
        gate_up(g)
    relay(2, 3)

    @pl.loop(0, n_mlp // 2)
    def _(k):
        g = (sibling + 2 * k) % n_mlp
        t_copy(g, mine, ts.at[0]).wait_recv()
        gate_up(g)

    def p_copy(g, src, c):
        return pltpu.make_async_remote_copy(
            src_ref=part.at[g, c], dst_ref=landed.at[src, c],
            send_sem=ps.at[g, c], recv_sem=pr.at[src, c], device_id={"mlp": g},
        )

    def nth(k):
        second = jnp.where(za == 0, 1, za - 1)
        third_a = jnp.where(za == 3, 1, jnp.where(za == 2, 3, 2))
        fourth = jnp.where(za < 2, 3, 0)
        return jnp.where(k == 0, za, jnp.where(k == 1, second, jnp.where(k == 2, third_a, fourth)))

    @pl.loop(0, LINE)
    def _(k):
        a = nth(k)
        y_wait(2, a)

        @pl.loop(1, n_mlp + 1)
        def _(j):
            g = (mine + j) % n_mlp
            part[g, a] = lax.dot_general(
                hidden[g], w_all[2, pl.ds(pl.multiple_of(a * chunk, 16), chunk)],
                (((1,), (1,)), ((), ())), preferred_element_type=jnp.float32,
            ).astype(jnp.bfloat16)

            @pl.when(j < n_mlp)
            def _():
                p_copy(g, mine, a).start()

    @pl.loop(0, LINE)
    def _(k):
        a = nth(k)
        cols = pl.ds(pl.multiple_of(a * chunk, 128), chunk)
        total = part[mine, a].astype(jnp.float32)
        for g in others:
            p_copy(mine, g, a).wait_recv()
            total = total + landed[g, a].astype(jnp.float32)
        out_ref[:, cols] = (out_ref[:, cols].astype(jnp.float32) + total).astype(jnp.bfloat16)

    for toward in alike + [sibling]:
        t_copy(mine, toward, ts.at[toward]).wait_send()
    for owner in alike:
        t_copy(owner, sibling, tf.at[owner]).wait_send()

    @pl.loop(0, LINE)
    def _(a):
        for g in others:
            p_copy(g, mine, a).wait_send()

    for w in range(3):
        if not early:
            own(w, True)
        for dist in range(2 if early and w == 0 else 1, LINE):
            relay(w, dist, True)
    if not early:
        @pl.loop(0, 3)
        def _(w):
            @pl.loop(0, LINE)
            def _(a):
                for dist in range(1, cross):
                    for side in (-1, 1):
                        origin = yb + side * dist

                        @pl.when((origin >= 0) & (origin < cross))
                        def _():
                            y_send(w, a, origin, (-side,), True)


EARLY_BLOCKS = [
    (0, 0, 1), (0, -1, 0), (0, 1, 0), (1, 0, 1), (1, -1, 0), (1, 1, 0),
    (0, -1, 1), (0, 1, 1), (0, -2, 0), (0, 2, 0),
]


def early_blocks(w_gate, w_up, w_down):
    requests = lax.axis_size("req")
    cross = requests // LINE
    if cross != 2:
        return []
    swap = [(r, r ^ 1) for r in range(requests)]
    ahead = [(r, r + cross) for r in range(requests - cross)]
    back = [(r + cross, r) for r in range(requests - cross)]
    send = functools.partial(lax.ppermute, axis_name="req")
    gate = w_gate[None]
    pair = jnp.stack([w_up, w_down])
    gate_low, gate_high = send(gate, perm=ahead), send(gate, perm=back)
    return [
        send(gate, perm=swap), gate_low, gate_high,
        send(pair, perm=swap), send(pair, perm=ahead), send(pair, perm=back),
        send(gate_low, perm=swap), send(gate_high, perm=swap),
        send(gate_low, perm=ahead), send(gate_high, perm=back),
    ]


def fused_layer(n_req, n_mlp, q, kv, ok, tokens, gain, w_out, w_gate, w_up, w_down, early):
    tok, model = tokens.shape
    depth, width = w_gate.shape
    chunk = model // LINE
    cross = n_req // LINE
    whole = pl.BlockSpec(memory_space=pltpu.VMEM)
    far = pl.BlockSpec(memory_space=pl.ANY)
    dma = pltpu.SemaphoreType.DMA
    half = jnp.bfloat16
    return pl.pallas_call(
        functools.partial(layer_kernel, (n_req, n_mlp, int(len(early) > 0))),
        out_shape=jax.ShapeDtypeStruct((tok, model), half),
        in_specs=[whole] * 5 + [far] * (4 + len(early)),
        out_specs=whole,
        scratch_shapes=[
            pltpu.VMEM((3, model, width), half),
            pltpu.VMEM(w_out.shape, half),
            pltpu.VMEM((tok, kv.shape[0]), jnp.float32),
            pltpu.VMEM((tok, HEADS * HD), half),
            pltpu.VMEM((n_mlp, tok, model), half),
            pltpu.VMEM((n_mlp, tok, width), half),
            pltpu.VMEM((n_mlp, LINE, tok, chunk), half),
            pltpu.VMEM((n_mlp, LINE, tok, chunk), half),
            dma((4 + 2 * N_EARLY,)),
            dma((3, LINE, 2)),
            dma((3, LINE)),
            dma((3, LINE, cross, 2)),
            dma((3, LINE, cross)),
            dma((n_mlp,)),
            dma((n_mlp,)),
            dma((n_mlp,)),
            dma((n_mlp, LINE)),
            dma((n_mlp, LINE)),
        ],
        compiler_params=pltpu.CompilerParams(
            collective_id=0, has_side_effects=True, vmem_limit_bytes=58 * 1024 * 1024
        ),
    )(q, kv, ok, tokens, gain, w_out, w_gate, w_up, w_down, *early)


def body(
    tokens, attn_gain, w_query, w_keyval, w_out, ffn_gain, w_gate, w_up, w_down,
    prefix_kv, own_prefix, leaf_parent, node_parent, seg_lengths,
):
    tok_rows = tokens.shape[0]
    requests = lax.axis_size("req")
    groups = lax.axis_size("mlp")
    mine = lax.axis_index("req")
    position_group = lax.axis_index("mlp")
    node_dev = prefix_kv.shape[1]
    seg_slot = prefix_kv.shape[2]
    leaf = leaf_parent[mine]
    upper = node_parent[leaf]
    len_zero = seg_lengths[0, upper]
    len_one = seg_lengths[1, leaf]
    len_two = seg_lengths[2, mine]
    total = len_zero + len_one + len_two

    early = early_blocks(w_gate, w_up, w_down)

    share = seg_slot // groups
    level_zero = node_parent[leaf_parent]
    wanted = jnp.stack([level_zero, leaf_parent], 1)
    owned = wanted // node_dev == mine
    local_slot = wanted % node_dev
    picker = (
        (local_slot[:, :, None] == jnp.arange(node_dev, dtype=jnp.int32)[None, None, :])
        & owned[:, :, None]
    ).astype(jnp.bfloat16)
    owners = wanted[mine] // node_dev
    from_owner = (jnp.arange(requests, dtype=jnp.int32)[:, None] == owners[None, :]).astype(
        jnp.bfloat16
    )
    shared_rows = lax.dynamic_slice_in_dim(prefix_kv, position_group * share, share, 2)
    outgoing = jnp.einsum(
        "rln,lnsc->rlsc", picker, shared_rows, preferred_element_type=jnp.float32
    ).astype(jnp.bfloat16)
    arrived = lax.all_to_all(outgoing, "req", split_axis=0, concat_axis=0, tiled=True)

    query_at = total + position_group * tok_rows + jnp.arange(tok_rows, dtype=jnp.int32)
    normed = rms_scale(tokens, attn_gain).astype(jnp.bfloat16)
    keyval_full = jnp.dot(normed, w_keyval, preferred_element_type=jnp.float32)
    new_keys = rotate(keyval_full[:, None, :HD], query_at)[:, 0].astype(jnp.bfloat16)
    new_vals = keyval_full[:, HD:].astype(jnp.bfloat16)
    new_keyval = jnp.concatenate([new_keys, new_vals], 1)
    query_full = jnp.dot(normed, w_query, preferred_element_type=jnp.float32).reshape(
        tok_rows, HEADS, HD
    )
    queries = (rotate(query_full, query_at) * HD ** (-0.5)).astype(jnp.bfloat16)

    levels = jnp.einsum(
        "rl,rlsc->lsc", from_owner, arrived, preferred_element_type=jnp.float32
    ).astype(jnp.bfloat16)
    gathered = lax.all_gather(
        jnp.concatenate([levels[0], levels[1], new_keyval], 0), "mlp", axis=0
    )
    cached = gathered[:, : 2 * share].reshape(groups, 2, share, 2 * HD)
    laid = jnp.zeros((WINDOW + 3 * seg_slot + groups * tok_rows, 2 * HD), jnp.bfloat16)
    laid = lax.dynamic_update_slice(laid, cached[:, 0].reshape(seg_slot, 2 * HD), (WINDOW, 0))
    laid = lax.dynamic_update_slice(
        laid, cached[:, 1].reshape(seg_slot, 2 * HD), (WINDOW + len_zero, 0)
    )
    laid = lax.dynamic_update_slice(laid, own_prefix[0], (WINDOW + len_zero + len_one, 0))
    laid = lax.dynamic_update_slice(
        laid, gathered[:, 2 * share :].reshape(groups * tok_rows, 2 * HD), (WINDOW + total, 0)
    )
    first = total + position_group * tok_rows
    keys = WINDOW + tok_rows
    window = lax.dynamic_slice_in_dim(laid, first, keys, 0)
    used = (first - WINDOW + jnp.arange(keys, dtype=jnp.int32) >= 0).astype(jnp.int32)[None, :]
    return fused_layer(
        requests, groups, queries.reshape(tok_rows, HEADS * HD), window, used, tokens,
        ffn_gain[None, :], w_out, w_gate, w_up, w_down, early,
    )


def solution(mesh):
    return jax.shard_map(
        body,
        mesh=mesh,
        in_specs=(
            P(("req", "mlp"), None),
            P(),
            P(),
            P(),
            P(),
            P(),
            P("req", "mlp"),
            P("req", "mlp"),
            P("req", "mlp"),
            P(None, "req", None, None),
            P("req", None, None),
            P(),
            P(),
            P(),
        ),
        out_specs=P(("req", "mlp"), None),
        check_vma=False,
    )
```

```python
import functools

import jax
import jax.numpy as jnp
from jax import lax
from jax.experimental import pallas as pl
from jax.experimental.pallas import tpu as pltpu
from jax.sharding import PartitionSpec as P

HEADS = 12
HD = 128
WINDOW = 1024


EPS = 1e-06


def rms_scale(values, gain):
    wide = values.astype(jnp.float32)
    return wide * lax.rsqrt(jnp.mean(wide * wide, axis=-1, keepdims=True) + EPS) * gain


def rotate(values, where_at):
    half_dim = values.shape[-1] // 2
    freqs = 10000.0 ** (-jnp.arange(half_dim, dtype=jnp.float32) / half_dim)
    angles = where_at.astype(jnp.float32)[:, None] * freqs[None, :]
    cosine = jnp.cos(angles)[:, None, :]
    sine = jnp.sin(angles)[:, None, :]
    first = values[..., :half_dim]
    second = values[..., half_dim:]
    return jnp.concatenate([first * cosine - second * sine, first * sine + second * cosine], -1)


LINE = 4
MASKED = -1e30
N_EARLY = 9


def layer_kernel(
    dims, q_ref, kv_ref, ok_ref, tok_ref, gain_ref, wout_hbm, wg_hbm, wu_hbm, wd_hbm, *rest
):
    early, rest = rest[:N_EARLY * dims[2]], rest[N_EARLY * dims[2]:]
    layer_steps(
        dims[:2], early, q_ref, kv_ref, ok_ref, tok_ref, gain_ref, wout_hbm, wg_hbm, wu_hbm,
        wd_hbm, *rest
    )


def layer_steps(
    dims, early, q_ref, kv_ref, ok_ref, tok_ref, gain_ref, wout_hbm, wg_hbm, wu_hbm, wd_hbm,
    out_ref, w_all, w_out, bias, ctx, rows_all, hidden, part, landed,
    load_sem, zs, zr, ys, yr, ts, tf, tr, ps, pr,
):
    n_req, n_mlp = dims
    cross = n_req // LINE
    me, mine = lax.axis_index("req"), lax.axis_index("mlp")
    za, yb = me // cross, me % cross
    depth = wg_hbm.shape[0]
    tok = tok_ref.shape[0]
    model = tok_ref.shape[1]
    chunk = model // LINE
    keys = kv_ref.shape[0]

    loads = [
        pltpu.make_async_copy(ref, w_all.at[w, pl.ds(pl.multiple_of(me * depth, 16), depth)], load_sem.at[w])
        for w, ref in enumerate((wg_hbm, wu_hbm, wd_hbm))
    ]
    loads.append(pltpu.make_async_copy(wout_hbm, w_out, load_sem.at[3]))
    for load in loads:
        load.start()

    ready = []
    for i, src in enumerate(early):
        kind = EARLY_BLOCKS[i]
        for j in range(src.shape[0]):
            a, b = za + kind[1], (1 - yb if kind[2] else yb)
            place = jnp.clip(a, 0, LINE - 1) * cross + b
            copy = pltpu.make_async_copy(
                src.at[j],
                w_all.at[kind[0] + j, pl.ds(pl.multiple_of(place * depth, 16), depth)],
                load_sem.at[4 + 2 * i + j],
            )
            ready.append(((a >= 0) & (a < LINE), copy))
    for there, copy in ready:
        @pl.when(there)
        def _():
            copy.start()

    barrier = pltpu.get_barrier_semaphore()
    for k in range(1, LINE):
        pl.semaphore_signal(barrier, inc=1, device_id={"req": ((za + k) % LINE) * cross + yb})
    for k in range(1, cross):
        pl.semaphore_signal(barrier, inc=1, device_id={"req": za * cross + (yb + k) % cross})
    for k in range(1, n_mlp):
        pl.semaphore_signal(barrier, inc=1, device_id={"mlp": (mine + k) % n_mlp})
    pl.semaphore_wait(barrier, LINE + cross + n_mlp - 3)

    def block(w, a, b):
        return w_all.at[w, pl.ds(pl.multiple_of((a * cross + b) * depth, 16), depth)]

    def z_copy(w, a, toward, side):
        return pltpu.make_async_remote_copy(
            src_ref=block(w, a, yb), dst_ref=block(w, a, yb),
            send_sem=zs.at[w, a, side], recv_sem=zr.at[w, a],
            device_id={"req": toward * cross + yb},
        )

    def y_copy(w, a, b, toward, side):
        return pltpu.make_async_remote_copy(
            src_ref=block(w, a, b), dst_ref=block(w, a, b),
            send_sem=ys.at[w, a, b, side], recv_sem=yr.at[w, a, b],
            device_id={"req": za * cross + toward},
        )

    def y_send(w, a, b, steps, finish=False):
        for step in steps:
            @pl.when((yb + step >= 0) & (yb + step < cross))
            def _():
                copy = y_copy(w, a, b, yb + step, (step + 1) // 2)
                copy.wait_send() if finish else copy.start()

    def z_send(w, a, steps, finish=False):
        for step in steps:
            @pl.when((za + step >= 0) & (za + step < LINE))
            def _():
                copy = z_copy(w, a, za + step, (step + 1) // 2)
                copy.wait_send() if finish else copy.start()

    def own(w, finish=False):
        z_send(w, za, (-1, 1), finish)
        y_send(w, za, yb, (-1, 1), finish)

    def relay(w, dist, finish=False):
        for side in (-1, 1):
            origin = za + side * dist

            @pl.when((origin >= 0) & (origin < LINE))
            def _():
                if not (finish or (early and dist == 1)):
                    z_copy(w, origin, za, 0).wait_recv()
                z_send(w, origin, (-side,), finish)
                y_send(w, origin, yb, (-1, 1), finish)

    def y_wait(w, a):
        if early:
            @pl.when(a != za)
            def _():
                y_copy(w, a, 1 - yb, yb, 0).wait_recv()
            return
        for dist in range(1, cross):
            for side in (-1, 1):
                origin = yb + side * dist

                @pl.when((origin >= 0) & (origin < cross))
                def _():
                    y_copy(w, a, origin, yb, 0).wait_recv()
                    y_send(w, a, origin, (-side,))

    for load in loads[:3]:
        load.wait()
    for there, copy in ready:
        @pl.when(there)
        def _():
            copy.wait()
    if early:
        relay(0, 1)
        relay(1, 1)
    else:
        own(0)
        own(1)

    query_row = lax.broadcasted_iota(jnp.int32, (tok, keys), 0)
    slot = lax.broadcasted_iota(jnp.int32, (tok, keys), 1)
    allowed = (slot > query_row) & (slot <= query_row + WINDOW) & (ok_ref[...] > 0)
    bias[...] = jnp.where(allowed, 0.0, MASKED)

    def heads(first, count):
        @pl.loop(first, first + count)
        def _(h):
            cols = pl.ds(pl.multiple_of(h * HD, HD), HD)
            scores = lax.dot_general(
                q_ref[:, cols], kv_ref[:, :HD], (((1,), (1,)), ((), ())),
                preferred_element_type=jnp.float32,
            ) + bias[...]
            weights = jnp.exp(scores - jnp.max(scores, axis=-1, keepdims=True))
            denom = jnp.sum(weights, axis=-1, keepdims=True)
            mixed = jnp.dot(
                weights.astype(jnp.bfloat16), kv_ref[:, HD:], preferred_element_type=jnp.float32
            )
            ctx[:, cols] = (mixed / denom).astype(jnp.bfloat16)

    third = HEADS // 3
    heads(0, third)
    if early:
        relay(2, 1)
        relay(0, 2)
    else:
        relay(0, 1)
        relay(1, 1)
    heads(third, third)
    if early:
        relay(1, 2)
    else:
        own(2)
        relay(0, 2)
    heads(2 * third, HEADS - 2 * third)
    relay(0, 3) if early else relay(1, 2)
    loads[3].wait()

    @pl.loop(0, LINE)
    def _(c):
        cols = pl.ds(pl.multiple_of(c * chunk, 128), chunk)
        out_ref[:, cols] = (
            tok_ref[:, cols].astype(jnp.float32)
            + jnp.dot(ctx[...], w_out[:, cols], preferred_element_type=jnp.float32)
        ).astype(jnp.bfloat16)

    rows_all[mine] = rms_scale(out_ref[...], gain_ref[...]).astype(jnp.bfloat16)

    def t_copy(owner, toward, sem):
        return pltpu.make_async_remote_copy(
            src_ref=rows_all.at[owner], dst_ref=rows_all.at[owner],
            send_sem=sem, recv_sem=tr.at[owner], device_id={"mlp": toward},
        )

    others = [(mine + k) % n_mlp for k in range(1, n_mlp)]
    core = mine % 2
    sibling = mine + 1 - 2 * core
    alike = [(mine + 2 * k) % n_mlp for k in range(1, n_mlp // 2)]
    for toward in alike + [sibling]:
        t_copy(mine, toward, ts.at[toward]).start()
    if early:
        relay(2, 2)
        relay(1, 3)
    else:
        relay(2, 1)
        relay(0, 3)
        relay(1, 3)
        relay(2, 2)
    for owner in alike:
        t_copy(owner, mine, ts.at[0]).wait_recv()
        t_copy(owner, sibling, tf.at[owner]).start()
    for w in range(2):
        for a in range(LINE):
            y_wait(w, a)

    width = hidden.shape[2]
    tile = 384 if width % 384 == 0 else width

    def gate_up(g):
        for c in range(width // tile):
            cols = pl.ds(c * tile, tile)
            gate = jnp.dot(rows_all[g], w_all[0, :, cols], preferred_element_type=jnp.float32)
            upward = jnp.dot(rows_all[g], w_all[1, :, cols], preferred_element_type=jnp.float32)
            hidden[g, :, cols] = (jax.nn.gelu(gate, approximate=True) * upward).astype(jnp.bfloat16)

    gate_up(mine)
    for g in alike:
        gate_up(g)
    relay(2, 3)

    @pl.loop(0, n_mlp // 2)
    def _(k):
        g = (sibling + 2 * k) % n_mlp
        t_copy(g, mine, ts.at[0]).wait_recv()
        gate_up(g)

    def p_copy(g, src, c):
        return pltpu.make_async_remote_copy(
            src_ref=part.at[g, c], dst_ref=landed.at[src, c],
            send_sem=ps.at[g, c], recv_sem=pr.at[src, c], device_id={"mlp": g},
        )

    def nth(k):
        second = jnp.where(za == 0, 1, za - 1)
        third_a = jnp.where(za == 3, 1, jnp.where(za == 2, 3, 2))
        fourth = jnp.where(za < 2, 3, 0)
        return jnp.where(k == 0, za, jnp.where(k == 1, second, jnp.where(k == 2, third_a, fourth)))

    @pl.loop(0, LINE)
    def _(k):
        a = nth(k)
        y_wait(2, a)

        @pl.loop(1, n_mlp + 1)
        def _(j):
            g = (mine + j) % n_mlp
            part[g, a] = lax.dot_general(
                hidden[g], w_all[2, pl.ds(pl.multiple_of(a * chunk, 16), chunk)],
                (((1,), (1,)), ((), ())), preferred_element_type=jnp.float32,
            ).astype(jnp.bfloat16)

            @pl.when(j < n_mlp)
            def _():
                p_copy(g, mine, a).start()

    @pl.loop(0, LINE)
    def _(k):
        a = nth(k)
        cols = pl.ds(pl.multiple_of(a * chunk, 128), chunk)
        total = part[mine, a].astype(jnp.float32)
        for g in others:
            p_copy(mine, g, a).wait_recv()
            total = total + landed[g, a].astype(jnp.float32)
        out_ref[:, cols] = (out_ref[:, cols].astype(jnp.float32) + total).astype(jnp.bfloat16)

    for toward in alike + [sibling]:
        t_copy(mine, toward, ts.at[toward]).wait_send()
    for owner in alike:
        t_copy(owner, sibling, tf.at[owner]).wait_send()

    @pl.loop(0, LINE)
    def _(a):
        for g in others:
            p_copy(g, mine, a).wait_send()

    for w in range(3):
        if not early:
            own(w, True)
        for dist in range(1, LINE):
            relay(w, dist, True)
    if not early:
        @pl.loop(0, 3)
        def _(w):
            @pl.loop(0, LINE)
            def _(a):
                for dist in range(1, cross):
                    for side in (-1, 1):
                        origin = yb + side * dist

                        @pl.when((origin >= 0) & (origin < cross))
                        def _():
                            y_send(w, a, origin, (-side,), True)


EARLY_BLOCKS = [
    (w, step, other) for w in range(3) for step, other in ((0, 1), (-1, 0), (1, 0))
]


def early_blocks(w_gate, w_up, w_down):
    requests = lax.axis_size("req")
    cross = requests // LINE
    if cross != 2:
        return []
    swap = [(r, r ^ 1) for r in range(requests)]
    ahead = [(r, r + cross) for r in range(requests - cross)]
    back = [(r + cross, r) for r in range(requests - cross)]
    send = functools.partial(lax.ppermute, axis_name="req")
    return [
        send(shard[None], perm=perm)
        for shard in (w_gate, w_up, w_down)
        for perm in (swap, ahead, back)
    ]


def fused_layer(n_req, n_mlp, q, kv, ok, tokens, gain, w_out, w_gate, w_up, w_down, early):
    tok, model = tokens.shape
    depth, width = w_gate.shape
    chunk = model // LINE
    cross = n_req // LINE
    whole = pl.BlockSpec(memory_space=pltpu.VMEM)
    far = pl.BlockSpec(memory_space=pl.ANY)
    dma = pltpu.SemaphoreType.DMA
    half = jnp.bfloat16
    return pl.pallas_call(
        functools.partial(layer_kernel, (n_req, n_mlp, int(len(early) > 0))),
        out_shape=jax.ShapeDtypeStruct((tok, model), half),
        in_specs=[whole] * 5 + [far] * (4 + len(early)),
        out_specs=whole,
        scratch_shapes=[
            pltpu.VMEM((3, model, width), half),
            pltpu.VMEM(w_out.shape, half),
            pltpu.VMEM((tok, kv.shape[0]), jnp.float32),
            pltpu.VMEM((tok, HEADS * HD), half),
            pltpu.VMEM((n_mlp, tok, model), half),
            pltpu.VMEM((n_mlp, tok, width), half),
            pltpu.VMEM((n_mlp, LINE, tok, chunk), half),
            pltpu.VMEM((n_mlp, LINE, tok, chunk), half),
            dma((4 + 2 * N_EARLY,)),
            dma((3, LINE, 2)),
            dma((3, LINE)),
            dma((3, LINE, cross, 2)),
            dma((3, LINE, cross)),
            dma((n_mlp,)),
            dma((n_mlp,)),
            dma((n_mlp,)),
            dma((n_mlp, LINE)),
            dma((n_mlp, LINE)),
        ],
        compiler_params=pltpu.CompilerParams(
            collective_id=0, has_side_effects=True, vmem_limit_bytes=58 * 1024 * 1024
        ),
    )(q, kv, ok, tokens, gain, w_out, w_gate, w_up, w_down, *early)


def body(
    tokens, attn_gain, w_query, w_keyval, w_out, ffn_gain, w_gate, w_up, w_down,
    prefix_kv, own_prefix, leaf_parent, node_parent, seg_lengths,
):
    tok_rows = tokens.shape[0]
    requests = lax.axis_size("req")
    groups = lax.axis_size("mlp")
    mine = lax.axis_index("req")
    position_group = lax.axis_index("mlp")
    node_dev = prefix_kv.shape[1]
    seg_slot = prefix_kv.shape[2]
    leaf = leaf_parent[mine]
    upper = node_parent[leaf]
    len_zero = seg_lengths[0, upper]
    len_one = seg_lengths[1, leaf]
    len_two = seg_lengths[2, mine]
    total = len_zero + len_one + len_two

    early = early_blocks(w_gate, w_up, w_down)

    share = seg_slot // groups
    level_zero = node_parent[leaf_parent]
    wanted = jnp.stack([level_zero, leaf_parent], 1)
    owned = wanted // node_dev == mine
    local_slot = wanted % node_dev
    picker = (
        (local_slot[:, :, None] == jnp.arange(node_dev, dtype=jnp.int32)[None, None, :])
        & owned[:, :, None]
    ).astype(jnp.bfloat16)
    owners = wanted[mine] // node_dev
    from_owner = (jnp.arange(requests, dtype=jnp.int32)[:, None] == owners[None, :]).astype(
        jnp.bfloat16
    )
    shared_rows = lax.dynamic_slice_in_dim(prefix_kv, position_group * share, share, 2)
    outgoing = jnp.einsum(
        "rln,lnsc->rlsc", picker, shared_rows, preferred_element_type=jnp.float32
    ).astype(jnp.bfloat16)
    arrived = lax.all_to_all(outgoing, "req", split_axis=0, concat_axis=0, tiled=True)

    query_at = total + position_group * tok_rows + jnp.arange(tok_rows, dtype=jnp.int32)
    normed = rms_scale(tokens, attn_gain).astype(jnp.bfloat16)
    keyval_full = jnp.dot(normed, w_keyval, preferred_element_type=jnp.float32)
    new_keys = rotate(keyval_full[:, None, :HD], query_at)[:, 0].astype(jnp.bfloat16)
    new_vals = keyval_full[:, HD:].astype(jnp.bfloat16)
    new_keyval = jnp.concatenate([new_keys, new_vals], 1)
    query_full = jnp.dot(normed, w_query, preferred_element_type=jnp.float32).reshape(
        tok_rows, HEADS, HD
    )
    queries = (rotate(query_full, query_at) * HD ** (-0.5)).astype(jnp.bfloat16)

    levels = jnp.einsum(
        "rl,rlsc->lsc", from_owner, arrived, preferred_element_type=jnp.float32
    ).astype(jnp.bfloat16)
    gathered = lax.all_gather(
        jnp.concatenate([levels[0], levels[1], new_keyval], 0), "mlp", axis=0
    )
    cached = gathered[:, : 2 * share].reshape(groups, 2, share, 2 * HD)
    laid = jnp.zeros((WINDOW + 3 * seg_slot + groups * tok_rows, 2 * HD), jnp.bfloat16)
    laid = lax.dynamic_update_slice(laid, cached[:, 0].reshape(seg_slot, 2 * HD), (WINDOW, 0))
    laid = lax.dynamic_update_slice(
        laid, cached[:, 1].reshape(seg_slot, 2 * HD), (WINDOW + len_zero, 0)
    )
    laid = lax.dynamic_update_slice(laid, own_prefix[0], (WINDOW + len_zero + len_one, 0))
    laid = lax.dynamic_update_slice(
        laid, gathered[:, 2 * share :].reshape(groups * tok_rows, 2 * HD), (WINDOW + total, 0)
    )
    first = total + position_group * tok_rows
    keys = WINDOW + tok_rows
    window = lax.dynamic_slice_in_dim(laid, first, keys, 0)
    used = (first - WINDOW + jnp.arange(keys, dtype=jnp.int32) >= 0).astype(jnp.int32)[None, :]
    return fused_layer(
        requests, groups, queries.reshape(tok_rows, HEADS * HD), window, used, tokens,
        ffn_gain[None, :], w_out, w_gate, w_up, w_down, early,
    )


def solution(mesh):
    return jax.shard_map(
        body,
        mesh=mesh,
        in_specs=(
            P(("req", "mlp"), None),
            P(),
            P(),
            P(),
            P(),
            P(),
            P("req", "mlp"),
            P("req", "mlp"),
            P("req", "mlp"),
            P(None, "req", None, None),
            P("req", None, None),
            P(),
            P(),
            P(),
        ),
        out_specs=P(("req", "mlp"), None),
        check_vma=False,
    )
```

```python
import functools

import jax
import jax.numpy as jnp
from jax import lax
from jax.experimental import pallas as pl
from jax.experimental.pallas import tpu as pltpu
from jax.sharding import PartitionSpec as P

HEADS = 12
HD = 128
WINDOW = 1024


EPS = 1e-06


def rms_scale(values, gain):
    wide = values.astype(jnp.float32)
    return wide * lax.rsqrt(jnp.mean(wide * wide, axis=-1, keepdims=True) + EPS) * gain


def rotate(values, where_at):
    half_dim = values.shape[-1] // 2
    freqs = 10000.0 ** (-jnp.arange(half_dim, dtype=jnp.float32) / half_dim)
    angles = where_at.astype(jnp.float32)[:, None] * freqs[None, :]
    cosine = jnp.cos(angles)[:, None, :]
    sine = jnp.sin(angles)[:, None, :]
    first = values[..., :half_dim]
    second = values[..., half_dim:]
    return jnp.concatenate([first * cosine - second * sine, first * sine + second * cosine], -1)


LINE = 4
MASKED = -1e30
N_EARLY = 9


def layer_kernel(
    dims, q_ref, kv_ref, ok_ref, tok_ref, gain_ref, wout_hbm, wg_hbm, wu_hbm, wd_hbm, *rest
):
    early, rest = rest[:N_EARLY * dims[2]], rest[N_EARLY * dims[2]:]
    layer_steps(
        dims[:2], early, q_ref, kv_ref, ok_ref, tok_ref, gain_ref, wout_hbm, wg_hbm, wu_hbm,
        wd_hbm, *rest
    )


def layer_steps(
    dims, early, q_ref, kv_ref, ok_ref, tok_ref, gain_ref, wout_hbm, wg_hbm, wu_hbm, wd_hbm,
    out_ref, w_all, w_out, bias, ctx, rows_all, hidden, part, landed,
    load_sem, zs, zr, ys, yr, ts, tf, tr, ps, pr,
):
    n_req, n_mlp = dims
    cross = n_req // LINE
    me, mine = lax.axis_index("req"), lax.axis_index("mlp")
    za, yb = me // cross, me % cross
    depth = wg_hbm.shape[0]
    tok = tok_ref.shape[0]
    model = tok_ref.shape[1]
    chunk = model // LINE
    keys = kv_ref.shape[0]

    loads = [
        pltpu.make_async_copy(ref, w_all.at[w, pl.ds(pl.multiple_of(me * depth, 16), depth)], load_sem.at[w])
        for w, ref in enumerate((wg_hbm, wu_hbm, wd_hbm))
    ]
    loads.append(pltpu.make_async_copy(wout_hbm, w_out, load_sem.at[3]))
    for load in loads:
        load.start()

    ready = []
    for i, src in enumerate(early):
        kind = EARLY_BLOCKS[i]
        for j in range(src.shape[0]):
            a, b = za + kind[1], (1 - yb if kind[2] else yb)
            place = jnp.clip(a, 0, LINE - 1) * cross + b
            copy = pltpu.make_async_copy(
                src.at[j],
                w_all.at[kind[0] + j, pl.ds(pl.multiple_of(place * depth, 16), depth)],
                load_sem.at[4 + 2 * i + j],
            )
            ready.append(((a >= 0) & (a < LINE), copy))
    for there, copy in ready:
        @pl.when(there)
        def _():
            copy.start()

    barrier = pltpu.get_barrier_semaphore()
    for k in range(1, LINE):
        pl.semaphore_signal(barrier, inc=1, device_id={"req": ((za + k) % LINE) * cross + yb})
    for k in range(1, cross):
        pl.semaphore_signal(barrier, inc=1, device_id={"req": za * cross + (yb + k) % cross})
    for k in range(1, n_mlp):
        pl.semaphore_signal(barrier, inc=1, device_id={"mlp": (mine + k) % n_mlp})
    pl.semaphore_wait(barrier, LINE + cross + n_mlp - 3)

    def block(w, a, b):
        return w_all.at[w, pl.ds(pl.multiple_of((a * cross + b) * depth, 16), depth)]

    def z_copy(w, a, toward, side):
        return pltpu.make_async_remote_copy(
            src_ref=block(w, a, yb), dst_ref=block(w, a, yb),
            send_sem=zs.at[w, a, side], recv_sem=zr.at[w, a],
            device_id={"req": toward * cross + yb},
        )

    def y_copy(w, a, b, toward, side):
        return pltpu.make_async_remote_copy(
            src_ref=block(w, a, b), dst_ref=block(w, a, b),
            send_sem=ys.at[w, a, b, side], recv_sem=yr.at[w, a, b],
            device_id={"req": za * cross + toward},
        )

    def y_send(w, a, b, steps, finish=False):
        for step in steps:
            @pl.when((yb + step >= 0) & (yb + step < cross))
            def _():
                copy = y_copy(w, a, b, yb + step, (step + 1) // 2)
                copy.wait_send() if finish else copy.start()

    def z_send(w, a, steps, finish=False):
        for step in steps:
            @pl.when((za + step >= 0) & (za + step < LINE))
            def _():
                copy = z_copy(w, a, za + step, (step + 1) // 2)
                copy.wait_send() if finish else copy.start()

    def own(w, finish=False):
        z_send(w, za, (-1, 1), finish)
        y_send(w, za, yb, (-1, 1), finish)

    def relay(w, dist, finish=False):
        for side in (-1, 1):
            origin = za + side * dist

            @pl.when((origin >= 0) & (origin < LINE))
            def _():
                if not (finish or (early and dist == 1)):
                    z_copy(w, origin, za, 0).wait_recv()
                z_send(w, origin, (-side,), finish)
                y_send(w, origin, yb, (-1, 1), finish)

    def y_wait(w, a):
        if early:
            @pl.when(a != za)
            def _():
                y_copy(w, a, 1 - yb, yb, 0).wait_recv()
            return
        for dist in range(1, cross):
            for side in (-1, 1):
                origin = yb + side * dist

                @pl.when((origin >= 0) & (origin < cross))
                def _():
                    y_copy(w, a, origin, yb, 0).wait_recv()
                    y_send(w, a, origin, (-side,))

    for load in loads[:3]:
        load.wait()
    for there, copy in ready:
        @pl.when(there)
        def _():
            copy.wait()
    if early:
        relay(0, 1)
        relay(1, 1)
    else:
        own(0)
        own(1)

    query_row = lax.broadcasted_iota(jnp.int32, (tok, keys), 0)
    slot = lax.broadcasted_iota(jnp.int32, (tok, keys), 1)
    allowed = (slot > query_row) & (slot <= query_row + WINDOW) & (ok_ref[...] > 0)
    bias[...] = jnp.where(allowed, 0.0, MASKED)

    def heads(first, count):
        @pl.loop(first, first + count)
        def _(h):
            cols = pl.ds(pl.multiple_of(h * HD, HD), HD)
            scores = lax.dot_general(
                q_ref[:, cols], kv_ref[:, :HD], (((1,), (1,)), ((), ())),
                preferred_element_type=jnp.float32,
            ) + bias[...]
            weights = jnp.exp(scores - jnp.max(scores, axis=-1, keepdims=True))
            denom = jnp.sum(weights, axis=-1, keepdims=True)
            mixed = jnp.dot(
                weights.astype(jnp.bfloat16), kv_ref[:, HD:], preferred_element_type=jnp.float32
            )
            ctx[:, cols] = (mixed / denom).astype(jnp.bfloat16)

    third = HEADS // 3
    heads(0, third)
    if early:
        relay(2, 1)
        relay(0, 2)
    else:
        relay(0, 1)
        relay(1, 1)
    heads(third, third)
    if early:
        relay(1, 2)
    else:
        own(2)
        relay(0, 2)
    heads(2 * third, HEADS - 2 * third)
    if not early:
        relay(1, 2)
    loads[3].wait()

    @pl.loop(0, LINE)
    def _(c):
        cols = pl.ds(pl.multiple_of(c * chunk, 128), chunk)
        out_ref[:, cols] = (
            tok_ref[:, cols].astype(jnp.float32)
            + jnp.dot(ctx[...], w_out[:, cols], preferred_element_type=jnp.float32)
        ).astype(jnp.bfloat16)

    rows_all[mine] = rms_scale(out_ref[...], gain_ref[...]).astype(jnp.bfloat16)

    def t_copy(owner, toward, sem):
        return pltpu.make_async_remote_copy(
            src_ref=rows_all.at[owner], dst_ref=rows_all.at[owner],
            send_sem=sem, recv_sem=tr.at[owner], device_id={"mlp": toward},
        )

    others = [(mine + k) % n_mlp for k in range(1, n_mlp)]
    core = mine % 2
    sibling = mine + 1 - 2 * core
    alike = [(mine + 2 * k) % n_mlp for k in range(1, n_mlp // 2)]
    for toward in alike + [sibling]:
        t_copy(mine, toward, ts.at[toward]).start()
    if early:
        relay(2, 2)
        relay(0, 3)
    else:
        relay(2, 1)
        relay(0, 3)
        relay(1, 3)
        relay(2, 2)
    for owner in alike:
        t_copy(owner, mine, ts.at[0]).wait_recv()
        t_copy(owner, sibling, tf.at[owner]).start()
    if early:
        relay(1, 3)
    for w in range(2):
        for a in range(LINE):
            y_wait(w, a)

    width = hidden.shape[2]
    tile = 384 if width % 384 == 0 else width

    def gate_up(g):
        for c in range(width // tile):
            cols = pl.ds(c * tile, tile)
            gate = jnp.dot(rows_all[g], w_all[0, :, cols], preferred_element_type=jnp.float32)
            upward = jnp.dot(rows_all[g], w_all[1, :, cols], preferred_element_type=jnp.float32)
            hidden[g, :, cols] = (jax.nn.gelu(gate, approximate=True) * upward).astype(jnp.bfloat16)

    gate_up(mine)
    for g in alike:
        gate_up(g)
    relay(2, 3)

    @pl.loop(0, n_mlp // 2)
    def _(k):
        g = (sibling + 2 * k) % n_mlp
        t_copy(g, mine, ts.at[0]).wait_recv()
        gate_up(g)

    def p_copy(g, src, c):
        return pltpu.make_async_remote_copy(
            src_ref=part.at[g, c], dst_ref=landed.at[src, c],
            send_sem=ps.at[g, c], recv_sem=pr.at[src, c], device_id={"mlp": g},
        )

    def nth(k):
        second = jnp.where(za == 0, 1, za - 1)
        third_a = jnp.where(za == 3, 1, jnp.where(za == 2, 3, 2))
        fourth = jnp.where(za < 2, 3, 0)
        return jnp.where(k == 0, za, jnp.where(k == 1, second, jnp.where(k == 2, third_a, fourth)))

    @pl.loop(0, LINE)
    def _(k):
        a = nth(k)
        y_wait(2, a)

        @pl.loop(1, n_mlp + 1)
        def _(j):
            g = (mine + j) % n_mlp
            part[g, a] = lax.dot_general(
                hidden[g], w_all[2, pl.ds(pl.multiple_of(a * chunk, 16), chunk)],
                (((1,), (1,)), ((), ())), preferred_element_type=jnp.float32,
            ).astype(jnp.bfloat16)

            @pl.when(j < n_mlp)
            def _():
                p_copy(g, mine, a).start()

    @pl.loop(0, LINE)
    def _(k):
        a = nth(k)
        cols = pl.ds(pl.multiple_of(a * chunk, 128), chunk)
        total = part[mine, a].astype(jnp.float32)
        for g in others:
            p_copy(mine, g, a).wait_recv()
            total = total + landed[g, a].astype(jnp.float32)
        out_ref[:, cols] = (out_ref[:, cols].astype(jnp.float32) + total).astype(jnp.bfloat16)

    for toward in alike + [sibling]:
        t_copy(mine, toward, ts.at[toward]).wait_send()
    for owner in alike:
        t_copy(owner, sibling, tf.at[owner]).wait_send()

    @pl.loop(0, LINE)
    def _(a):
        for g in others:
            p_copy(g, mine, a).wait_send()

    for w in range(3):
        if not early:
            own(w, True)
        for dist in range(1, LINE):
            relay(w, dist, True)
    if not early:
        @pl.loop(0, 3)
        def _(w):
            @pl.loop(0, LINE)
            def _(a):
                for dist in range(1, cross):
                    for side in (-1, 1):
                        origin = yb + side * dist

                        @pl.when((origin >= 0) & (origin < cross))
                        def _():
                            y_send(w, a, origin, (-side,), True)


EARLY_BLOCKS = [
    (w, step, other) for w in range(3) for step, other in ((0, 1), (-1, 0), (1, 0))
]


def early_blocks(w_gate, w_up, w_down):
    requests = lax.axis_size("req")
    cross = requests // LINE
    if cross != 2:
        return []
    swap = [(r, r ^ 1) for r in range(requests)]
    ahead = [(r, r + cross) for r in range(requests - cross)]
    back = [(r + cross, r) for r in range(requests - cross)]
    send = functools.partial(lax.ppermute, axis_name="req")
    return [
        send(shard[None], perm=perm)
        for shard in (w_gate, w_up, w_down)
        for perm in (swap, ahead, back)
    ]


def fused_layer(n_req, n_mlp, q, kv, ok, tokens, gain, w_out, w_gate, w_up, w_down, early):
    tok, model = tokens.shape
    depth, width = w_gate.shape
    chunk = model // LINE
    cross = n_req // LINE
    whole = pl.BlockSpec(memory_space=pltpu.VMEM)
    far = pl.BlockSpec(memory_space=pl.ANY)
    dma = pltpu.SemaphoreType.DMA
    half = jnp.bfloat16
    return pl.pallas_call(
        functools.partial(layer_kernel, (n_req, n_mlp, int(len(early) > 0))),
        out_shape=jax.ShapeDtypeStruct((tok, model), half),
        in_specs=[whole] * 5 + [far] * (4 + len(early)),
        out_specs=whole,
        scratch_shapes=[
            pltpu.VMEM((3, model, width), half),
            pltpu.VMEM(w_out.shape, half),
            pltpu.VMEM((tok, kv.shape[0]), jnp.float32),
            pltpu.VMEM((tok, HEADS * HD), half),
            pltpu.VMEM((n_mlp, tok, model), half),
            pltpu.VMEM((n_mlp, tok, width), half),
            pltpu.VMEM((n_mlp, LINE, tok, chunk), half),
            pltpu.VMEM((n_mlp, LINE, tok, chunk), half),
            dma((4 + 2 * N_EARLY,)),
            dma((3, LINE, 2)),
            dma((3, LINE)),
            dma((3, LINE, cross, 2)),
            dma((3, LINE, cross)),
            dma((n_mlp,)),
            dma((n_mlp,)),
            dma((n_mlp,)),
            dma((n_mlp, LINE)),
            dma((n_mlp, LINE)),
        ],
        compiler_params=pltpu.CompilerParams(
            collective_id=0, has_side_effects=True, vmem_limit_bytes=58 * 1024 * 1024
        ),
    )(q, kv, ok, tokens, gain, w_out, w_gate, w_up, w_down, *early)


def body(
    tokens, attn_gain, w_query, w_keyval, w_out, ffn_gain, w_gate, w_up, w_down,
    prefix_kv, own_prefix, leaf_parent, node_parent, seg_lengths,
):
    tok_rows = tokens.shape[0]
    requests = lax.axis_size("req")
    groups = lax.axis_size("mlp")
    mine = lax.axis_index("req")
    position_group = lax.axis_index("mlp")
    node_dev = prefix_kv.shape[1]
    seg_slot = prefix_kv.shape[2]
    leaf = leaf_parent[mine]
    upper = node_parent[leaf]
    len_zero = seg_lengths[0, upper]
    len_one = seg_lengths[1, leaf]
    len_two = seg_lengths[2, mine]
    total = len_zero + len_one + len_two

    early = early_blocks(w_gate, w_up, w_down)

    share = seg_slot // groups
    level_zero = node_parent[leaf_parent]
    wanted = jnp.stack([level_zero, leaf_parent], 1)
    owned = wanted // node_dev == mine
    local_slot = wanted % node_dev
    picker = (
        (local_slot[:, :, None] == jnp.arange(node_dev, dtype=jnp.int32)[None, None, :])
        & owned[:, :, None]
    ).astype(jnp.bfloat16)
    owners = wanted[mine] // node_dev
    from_owner = (jnp.arange(requests, dtype=jnp.int32)[:, None] == owners[None, :]).astype(
        jnp.bfloat16
    )
    shared_rows = lax.dynamic_slice_in_dim(prefix_kv, position_group * share, share, 2)
    outgoing = jnp.einsum(
        "rln,lnsc->rlsc", picker, shared_rows, preferred_element_type=jnp.float32
    ).astype(jnp.bfloat16)
    arrived = lax.all_to_all(outgoing, "req", split_axis=0, concat_axis=0, tiled=True)

    query_at = total + position_group * tok_rows + jnp.arange(tok_rows, dtype=jnp.int32)
    normed = rms_scale(tokens, attn_gain).astype(jnp.bfloat16)
    keyval_full = jnp.dot(normed, w_keyval, preferred_element_type=jnp.float32)
    new_keys = rotate(keyval_full[:, None, :HD], query_at)[:, 0].astype(jnp.bfloat16)
    new_vals = keyval_full[:, HD:].astype(jnp.bfloat16)
    new_keyval = jnp.concatenate([new_keys, new_vals], 1)
    query_full = jnp.dot(normed, w_query, preferred_element_type=jnp.float32).reshape(
        tok_rows, HEADS, HD
    )
    queries = (rotate(query_full, query_at) * HD ** (-0.5)).astype(jnp.bfloat16)

    levels = jnp.einsum(
        "rl,rlsc->lsc", from_owner, arrived, preferred_element_type=jnp.float32
    ).astype(jnp.bfloat16)
    gathered = lax.all_gather(
        jnp.concatenate([levels[0], levels[1], new_keyval], 0), "mlp", axis=0
    )
    cached = gathered[:, : 2 * share].reshape(groups, 2, share, 2 * HD)
    laid = jnp.zeros((WINDOW + 3 * seg_slot + groups * tok_rows, 2 * HD), jnp.bfloat16)
    laid = lax.dynamic_update_slice(laid, cached[:, 0].reshape(seg_slot, 2 * HD), (WINDOW, 0))
    laid = lax.dynamic_update_slice(
        laid, cached[:, 1].reshape(seg_slot, 2 * HD), (WINDOW + len_zero, 0)
    )
    laid = lax.dynamic_update_slice(laid, own_prefix[0], (WINDOW + len_zero + len_one, 0))
    laid = lax.dynamic_update_slice(
        laid, gathered[:, 2 * share :].reshape(groups * tok_rows, 2 * HD), (WINDOW + total, 0)
    )
    first = total + position_group * tok_rows
    keys = WINDOW + tok_rows
    window = lax.dynamic_slice_in_dim(laid, first, keys, 0)
    used = (first - WINDOW + jnp.arange(keys, dtype=jnp.int32) >= 0).astype(jnp.int32)[None, :]
    return fused_layer(
        requests, groups, queries.reshape(tok_rows, HEADS * HD), window, used, tokens,
        ffn_gain[None, :], w_out, w_gate, w_up, w_down, early,
    )


def solution(mesh):
    return jax.shard_map(
        body,
        mesh=mesh,
        in_specs=(
            P(("req", "mlp"), None),
            P(),
            P(),
            P(),
            P(),
            P(),
            P("req", "mlp"),
            P("req", "mlp"),
            P("req", "mlp"),
            P(None, "req", None, None),
            P("req", None, None),
            P(),
            P(),
            P(),
        ),
        out_specs=P(("req", "mlp"), None),
        check_vma=False,
    )
```
